32 devices in a mesh: sec: 2 (over x), dp: 8 (over z, core), mp: 2 (over y).
Axes of the slice: x: 2, y: 2, z: 4, core: 2. Of those that a mesh axis runs over, the one named last changes fastest.
Arguments:
- queries: bfloat16 [64, 128, 4096], P(('sec', 'dp'), None, 'mp'), may hold values from -12 to 12
- keys_values: bfloat16 [256, 2, 32, 4096], P(('sec', 'dp'), None, None, 'mp'), may hold values from -5.5 to 5.5
- cotangent: bfloat16 [64, 128, 4096], P(('sec', 'dp'), None, 'mp'), may hold values from -4 to 4
- passage_slot: int32 [256], replicated, may hold values from 0 to 31, as said below
- passage_question: int32 [256], replicated, may hold values from 0 to 3, as said below
Outputs:
- grad_queries: bfloat16 [64, 128, 4096], P(('sec', 'dp'), None, 'mp')
- grad_keys_values: bfloat16 [256, 2, 32, 4096], P(('sec', 'dp'), None, None, 'mp')
- relevance: bfloat16 [256], P(('sec', 'dp'))
The draws below stay inside these ranges and needn't reach their ends.
Inputs may be any that keep to these rules, and one draw needn't show every extreme that they name: A passage of section s goes to decoder device passage_slot // 4 of the other section, into its slot passage_slot % 4 for that encoder device. The passages of one device name distinct values, so one encoder device sends at most 4 passages to one decoder device, and every encoder device sends exactly 4 to some decoder device. `passage_question`: the question, among the 4 questions of its decoder device, that a passage serves; every question has at least one passage.
All inputs are finite; a program needn't handle non-finite values.
Results may differ from the reference program's by a relative error of at most 0.0014.
The reference program's roundings to bfloat16 on the way (of `rounded_prob` and `grad_score`) count: a program that leaves them out, or rounds other values in their place, can miss the bound.
Values may be sent and summed in bfloat16 or wider, within the bound.
A program may use at most 192 MiB of HBM per device.

```python
import math
import jax
import jax.numpy as jnp
from jax import lax

D = 4096
HEADS = 64
HD = 64
P_DEV = 16
Q_DEV = 4
PLEN = 32
ANS = 128
SLOTS = 32
PASSAGES = 256
QUESTIONS = 64
N_SEC = 2
N_DP = 8


def draw_queries(key, part):
    scale_key, normal_key = jax.random.split(jax.random.fold_in(key, 101), 2)
    head_count = D // HD
    head_scale = jnp.exp(jax.random.uniform(scale_key, (head_count,), jnp.float32, math.log(0.3), math.log(3.0)))
    values = jnp.clip(jax.random.normal(normal_key, (QUESTIONS, ANS, D), jnp.float32), -4.0, 4.0)
    values = values * jnp.repeat(head_scale, HD)[None, None, :]
    return values.astype(jnp.bfloat16)


def draw_keys_values(key, part):
    normal_key = jax.random.fold_in(jax.random.fold_in(key, 202), 0)
    values = jnp.clip(jax.random.normal(normal_key, (PASSAGES, 2, PLEN, D), jnp.float32), -4.0, 4.0)
    return values.astype(jnp.bfloat16)


def route_tables(key):
    route_key = jax.random.fold_in(key, 303)
    preference_key, jitter_key, pick_key, shuffle_key = jax.random.split(route_key, 4)
    encoders = PASSAGES // P_DEV
    n_devices = encoders // 2
    per_pair = SLOTS // n_devices
    reach_count = Q_DEV // per_pair
    extra_count = P_DEV - Q_DEV
    device_of = jnp.arange(encoders, dtype=jnp.int32) % n_devices
    target = 1 - jnp.arange(encoders, dtype=jnp.int32) // n_devices
    columns = jnp.arange(SLOTS, dtype=jnp.int32)
    column_owner = columns // per_pair
    offset = (column_owner[None, :] - device_of[:, None]) % n_devices
    preference = jax.random.randint(preference_key, (2, n_devices), 0, 2 ** 20, dtype=jnp.int32)
    preference_rows = preference[target][:, column_owner]
    jitter = jax.random.randint(jitter_key, (encoders, SLOTS), 0, 2 ** 19, dtype=jnp.int32)
    scores = (preference_rows + jitter) * SLOTS + columns[None, :]
    scores = jnp.where(offset < reach_count, -1, scores)
    picked = lax.top_k(scores, extra_count)[1].astype(jnp.int32)
    base_index = jnp.arange(Q_DEV, dtype=jnp.int32)
    base_columns = (device_of[:, None] + base_index[None, :] // per_pair) % n_devices * per_pair + base_index[None, :] % per_pair
    slot_table = jnp.concatenate([base_columns, picked], 1)
    extra_questions = jax.random.randint(pick_key, (encoders, extra_count), 0, Q_DEV, dtype=jnp.int32)
    question_table = jnp.concatenate([jnp.broadcast_to(base_index[None, :], (encoders, Q_DEV)), extra_questions], 1)
    shuffle_scores = jax.random.randint(shuffle_key, (encoders, P_DEV), 0, 2 ** 20, dtype=jnp.int32) * P_DEV + jnp.arange(P_DEV, dtype=jnp.int32)[None, :]
    shuffle = jnp.argsort(shuffle_scores, axis=1)
    slot_table = jnp.take_along_axis(slot_table, shuffle, 1)
    question_table = jnp.take_along_axis(question_table, shuffle, 1)
    return (slot_table.reshape(-1).astype(jnp.int32), question_table.reshape(-1).astype(jnp.int32))


def draw_passage_slot(key, part):
    return route_tables(key)[0]


def draw_passage_question(key, part):
    return route_tables(key)[1]


def block_scale(stream_key, dims, shards, least, largest):
    def one(axis_at, parts):
        steps = jax.random.uniform(jax.random.fold_in(jax.random.fold_in(stream_key, 6), axis_at), (parts,), jnp.float32, least / len(shards), largest / len(shards))
        return jnp.repeat(jnp.exp(steps), dims[axis_at] // parts).reshape((-1,) + (1,) * (len(dims) - axis_at - 1))

    level = one(*shards[0])
    for cut in shards[1:]:
        level = level * one(*cut)
    return level


def bell_draw(stream_key, shape, width, limit, pieces=(), kind=jnp.bfloat16):
    result = width * jax.random.normal(stream_key, shape, jnp.float32)
    if pieces:
        result = result * block_scale(stream_key, shape, pieces, -0.22, 0.18)
    return jnp.clip(result, -limit, limit).astype(kind)


def setup_inputs(seed: int = 0) -> dict:
    streams_of = jax.random.split(jax.random.key(seed), 6)
    return {
        "queries": draw_queries(jax.random.fold_in(streams_of[5], 71), 0),
        "keys_values": draw_keys_values(jax.random.fold_in(streams_of[5], 71), 0),
        "cotangent": bell_draw(streams_of[2], (QUESTIONS, ANS, D), 1.0, 4.0, ((0, 16), (2, 2))),
        "passage_slot": draw_passage_slot(jax.random.fold_in(streams_of[5], 71), 0),
        "passage_question": draw_passage_question(jax.random.fold_in(streams_of[5], 71), 0),
    }


def rounded(values):
    return lax.optimization_barrier(values.astype(jnp.bfloat16)).astype(jnp.float32)

def attend_all(query_block, grad_block, slot_tiles, owners):
    head_count = D // HD
    row_count = Q_DEV * ANS
    key_count = SLOTS * PLEN
    score_scale = 1.0 / math.sqrt(HD)
    query_heads = query_block.reshape(row_count, head_count, HD).astype(jnp.float32)
    grad_heads = grad_block.reshape(row_count, head_count, HD).astype(jnp.float32)
    key_heads = slot_tiles[:, 0].reshape(key_count, head_count, HD).astype(jnp.float32)
    value_heads = slot_tiles[:, 1].reshape(key_count, head_count, HD).astype(jnp.float32)
    row_owner = jnp.arange(row_count, dtype=jnp.int32) // ANS
    key_owner = jnp.repeat(owners, PLEN)
    allowed = row_owner[:, None] == key_owner[None, :]
    scores = jnp.einsum('rhc,khc->hrk', query_heads, key_heads) * score_scale
    scores = jnp.where(allowed[None], scores, -jnp.inf)
    row_max = lax.optimization_barrier(jnp.max(scores, -1, keepdims=True))
    exponent = jnp.exp(scores - row_max)
    probability = exponent / lax.optimization_barrier(jnp.sum(exponent, -1, keepdims=True))
    rounded_prob = rounded(probability)
    attended = jnp.einsum('hrk,khc->hrc', rounded_prob, value_heads)
    grad_prob = jnp.einsum('rhc,khc->hrk', grad_heads, value_heads)
    row_delta = jnp.einsum('rhc,hrc->hr', grad_heads, attended)
    grad_score = rounded(probability * (grad_prob - row_delta[..., None]))
    grad_query = (jnp.einsum('hrk,khc->rhc', grad_score, key_heads) * score_scale).astype(jnp.bfloat16)
    grad_key = (jnp.einsum('hrk,rhc->khc', grad_score, query_heads) * score_scale).astype(jnp.bfloat16)
    grad_value = jnp.einsum('hrk,rhc->khc', rounded_prob, grad_heads).astype(jnp.bfloat16)
    grad_tiles = jnp.stack([grad_key.reshape(SLOTS, PLEN, D), grad_value.reshape(SLOTS, PLEN, D)], 1)
    head_mass = lax.optimization_barrier(jnp.sum(probability, (0, 1))).reshape(SLOTS, PLEN).sum(-1)
    return (grad_query.reshape(Q_DEV, ANS, D), grad_tiles, head_mass)

def reference(queries, keys_values, cotangent, passage_slot, passage_question):
    per_pair = SLOTS // N_DP

    def serve(running, decoder_index):
        grad_tiles, relevance = running
        section = decoder_index // N_DP
        decoder = decoder_index % N_DP
        source = 1 - section
        source_start = (source * N_DP * P_DEV).astype(jnp.int32)
        table_slot = lax.dynamic_slice_in_dim(passage_slot, source_start, N_DP * P_DEV).reshape(N_DP, P_DEV)
        table_question = lax.dynamic_slice_in_dim(passage_question, source_start, N_DP * P_DEV).reshape(N_DP, P_DEV)
        wanted = decoder * per_pair + jnp.arange(per_pair, dtype=jnp.int32)
        matches = table_slot[:, None, :] == wanted[None, :, None]
        present = jnp.any(matches, -1).reshape(SLOTS)
        position = lax.optimization_barrier(jnp.sum(jnp.where(matches, jnp.arange(P_DEV, dtype=jnp.int32)[None, None, :], 0), -1))
        passage_index = (source_start + jnp.arange(N_DP, dtype=jnp.int32)[:, None] * P_DEV + position).reshape(SLOTS).astype(jnp.int32)
        owner_ids = lax.optimization_barrier(jnp.sum(jnp.where(matches, table_question[:, None, :], 0), -1)).reshape(SLOTS)
        owners = jnp.where(present, owner_ids, -1).astype(jnp.int32)
        slot_tiles = jnp.where(present[:, None, None, None], keys_values[passage_index], jnp.zeros((), keys_values.dtype))
        query_block = lax.dynamic_slice_in_dim(queries, (decoder_index * Q_DEV).astype(jnp.int32), Q_DEV)
        grad_block = lax.dynamic_slice_in_dim(cotangent, (decoder_index * Q_DEV).astype(jnp.int32), Q_DEV)
        grad_query, grad_slot, head_mass = attend_all(query_block, grad_block, slot_tiles, owners)
        slot_relevance = (head_mass / (HEADS * ANS)).astype(jnp.bfloat16)
        grad_slot = jnp.where(present[:, None, None, None], grad_slot, jnp.zeros((), grad_slot.dtype))
        slot_relevance = jnp.where(present, slot_relevance, jnp.zeros((), slot_relevance.dtype))
        grad_tiles = grad_tiles.at[passage_index].add(grad_slot)
        relevance = relevance.at[passage_index].add(slot_relevance)
        return ((grad_tiles, relevance), grad_query)
    start_state = (jnp.zeros((PASSAGES, 2, PLEN, D), jnp.bfloat16), jnp.zeros((PASSAGES,), jnp.bfloat16))
    final_state, grad_queries = lax.scan(serve, start_state, jnp.arange(N_SEC * N_DP, dtype=jnp.int32))
    grad_tiles, relevance = final_state
    return (grad_queries.reshape(QUESTIONS, ANS, D), grad_tiles, relevance)
```

```python
import functools
import math

import jax
import jax.numpy as jnp
from jax import lax
from jax.experimental import pallas as pl
from jax.experimental.pallas import tpu as pltpu
from jax.sharding import PartitionSpec as P

HEADS = 64
HD = 64
ANS = 128
SLOTS = 32
LANES = 128
CHUNKS = 4
GROUP = 8
MESH = pl.DeviceIdType.MESH
VMEM_LIMIT = 48 * 1024 * 1024


def remote(src, dst, send_sem, recv_sem, where):
    return pltpu.make_async_remote_copy(
        src_ref=src,
        dst_ref=dst,
        send_sem=send_sem,
        recv_sem=recv_sem,
        device_id=where,
        device_id_type=MESH,
    )


def greet(targets):
    barrier = pltpu.get_barrier_semaphore()
    for where in targets:
        pl.semaphore_signal(barrier, inc=1, device_id=where, device_id_type=MESH)
    pl.semaphore_wait(barrier, len(targets))


def dispatch_kernel(
    n, index_ref, kv_ref, recv_ref, mid, out, x_send, x_recv, z_send, z_recv, own_sem
):
    section = lax.axis_index("sec")
    me = lax.axis_index("dp")
    per_pair = SLOTS // n
    columns = kv_ref.shape[3] // CHUNKS
    peers = [lax.rem(me + d, n) for d in range(1, n)]
    across = {"sec": 1 - section}
    greet([across] + [{"dp": peer} for peer in peers])

    crossing = []
    for c in range(CHUNKS):
        copy = remote(
            kv_ref.at[:, :, :, pl.ds(c * columns, columns)],
            mid[c],
            x_send.at[c],
            x_recv.at[c],
            across,
        )
        copy.start()
        crossing.append(copy)
    sends = []
    locals_ = []
    my_rows = pl.ds(me * per_pair, per_pair)
    for c in range(CHUNKS):
        crossing[c].wait_recv()

        def place(s, carry):
            out[c, s] = mid[c][index_ref[s]]
            return carry

        lax.fori_loop(0, SLOTS, place, 0)
        for d, peer in enumerate(peers, 1):
            copy = remote(
                out.at[c, pl.ds(peer * per_pair, per_pair)],
                recv_ref.at[c, my_rows],
                z_send.at[c, d],
                z_recv.at[c, d],
                {"dp": peer},
            )
            copy.start()
            sends.append(copy)
        copy = pltpu.make_async_copy(out.at[c, my_rows], recv_ref.at[c, my_rows], own_sem.at[c])
        copy.start()
        locals_.append(copy)
    for c in range(CHUNKS):
        crossing[c].wait_send()
        locals_[c].wait()
        for d in range(1, n):
            source = lax.rem(me + n - d, n)
            landed = recv_ref.at[c, pl.ds(source * per_pair, per_pair)]
            remote(landed, landed, z_send.at[c, d], z_recv.at[c, d], {"dp": source}).wait_recv()
    for copy in sends:
        copy.wait_send()


def dispatch(keys_values, index):
    n = lax.axis_size("dp")
    count, _, rows, width = keys_values.shape
    columns = width // CHUNKS
    return pl.pallas_call(
        functools.partial(dispatch_kernel, n),
        out_shape=jax.ShapeDtypeStruct((CHUNKS, SLOTS, 2, rows, columns), jnp.bfloat16),
        in_specs=[
            pl.BlockSpec(memory_space=pltpu.SMEM),
            pl.BlockSpec(memory_space=pl.ANY),
        ],
        out_specs=pl.BlockSpec(memory_space=pl.ANY),
        scratch_shapes=[
            [pltpu.VMEM((count, 2, rows, columns), jnp.bfloat16)] * CHUNKS,
            pltpu.VMEM((CHUNKS, SLOTS, 2, rows, columns), jnp.bfloat16),
            pltpu.SemaphoreType.DMA((CHUNKS,)),
            pltpu.SemaphoreType.DMA((CHUNKS,)),
            pltpu.SemaphoreType.DMA((CHUNKS, n)),
            pltpu.SemaphoreType.DMA((CHUNKS, n)),
            pltpu.SemaphoreType.DMA((CHUNKS,)),
        ],
        compiler_params=pltpu.CompilerParams(
            collective_id=0, has_side_effects=True, vmem_limit_bytes=VMEM_LIMIT
        ),
    )(index, keys_values)


def collect_kernel(
    n,
    slot_ref,
    grads_ref,
    mass_ref,
    tiles_ref,
    total_ref,
    back,
    dense,
    mass_back,
    mass_dense,
    mass_here,
    mass_other,
    z_send,
    z_recv,
    own_sem,
    x_send,
    x_recv,
    m_send,
    m_recv,
    small_send,
    small_recv,
):
    section = lax.axis_index("sec")
    me = lax.axis_index("dp")
    half = lax.axis_index("mp")
    per_pair = SLOTS // n
    count = dense.shape[1]
    columns = dense.shape[4]
    peers = [lax.rem(me + d, n) for d in range(1, n)]
    across = {"sec": 1 - section}
    beside = {"mp": 1 - half}
    greet([across, beside] + [{"dp": peer} for peer in peers])

    my_rows = pl.ds(me * per_pair, per_pair)
    sends = []
    locals_ = []
    for d, peer in enumerate(peers, 1):
        copy = remote(
            mass_ref.at[pl.ds(peer * per_pair, per_pair)],
            mass_back.at[my_rows],
            m_send.at[d],
            m_recv.at[d],
            {"dp": peer},
        )
        copy.start()
        sends.append(copy)
    own_mass = pltpu.make_async_copy(mass_ref.at[my_rows], mass_back.at[my_rows], own_sem.at[CHUNKS])
    own_mass.start()
    for c in range(CHUNKS):
        for d, peer in enumerate(peers, 1):
            copy = remote(
                grads_ref.at[c, pl.ds(peer * per_pair, per_pair)],
                back[c].at[my_rows],
                z_send.at[c, d],
                z_recv.at[c, d],
                {"dp": peer},
            )
            copy.start()
            sends.append(copy)
        copy = pltpu.make_async_copy(grads_ref.at[c, my_rows], back[c].at[my_rows], own_sem.at[c])
        copy.start()
        locals_.append(copy)

    def arrived(buffer, send_sem, recv_sem, d):
        source = lax.rem(me + n - d, n)
        landed = buffer.at[pl.ds(source * per_pair, per_pair)]
        remote(landed, landed, send_sem, recv_sem, {"dp": source}).wait_recv()

    own_mass.wait()
    for d in range(1, n):
        arrived(mass_back, m_send.at[d], m_recv.at[d], d)

    def pick_mass(j, carry):
        mass_dense[j] = mass_back[slot_ref[j]]
        return carry

    lax.fori_loop(0, count, pick_mass, 0)
    first = remote(mass_dense, mass_here, small_send.at[0], small_recv.at[0], across)
    first.start()

    crossing = []
    second = None
    for c in range(CHUNKS):
        locals_[c].wait()
        for d in range(1, n):
            arrived(back[c], z_send.at[c, d], z_recv.at[c, d], d)

        def pick(j, carry):
            dense[c, j] = back[c][slot_ref[j]]
            return carry

        lax.fori_loop(0, count, pick, 0)
        copy = remote(
            dense.at[c],
            tiles_ref.at[:, :, :, pl.ds(c * columns, columns)],
            x_send.at[c],
            x_recv.at[c],
            across,
        )
        copy.start()
        crossing.append(copy)
        if c == 0:
            first.wait_recv()
            second = remote(mass_here, mass_other, small_send.at[1], small_recv.at[1], beside)
            second.start()
    second.wait()
    total_ref[...] = mass_here[...] + mass_other[...]
    first.wait_send()
    for copy in crossing:
        copy.wait()
    for copy in sends:
        copy.wait_send()


def collect(slots, grads, mass, count):
    n = lax.axis_size("dp")
    _, _, _, rows, columns = grads.shape
    small = pltpu.VMEM((count, 8, LANES), jnp.float32)
    return pl.pallas_call(
        functools.partial(collect_kernel, n),
        out_shape=(
            jax.ShapeDtypeStruct((count, 2, rows, columns * CHUNKS), jnp.bfloat16),
            jax.ShapeDtypeStruct((count, 8, LANES), jnp.float32),
        ),
        in_specs=[
            pl.BlockSpec(memory_space=pltpu.SMEM),
            pl.BlockSpec(memory_space=pl.ANY),
            pl.BlockSpec(memory_space=pl.ANY),
        ],
        out_specs=(
            pl.BlockSpec(memory_space=pl.ANY),
            pl.BlockSpec(memory_space=pltpu.VMEM),
        ),
        scratch_shapes=[
            [pltpu.VMEM((SLOTS, 2, rows, columns), jnp.bfloat16)] * CHUNKS,
            pltpu.VMEM((CHUNKS, count, 2, rows, columns), jnp.bfloat16),
            pltpu.VMEM((SLOTS, 8, LANES), jnp.float32),
            small,
            small,
            small,
            pltpu.SemaphoreType.DMA((CHUNKS, n)),
            pltpu.SemaphoreType.DMA((CHUNKS, n)),
            pltpu.SemaphoreType.DMA((CHUNKS + 1,)),
            pltpu.SemaphoreType.DMA((CHUNKS,)),
            pltpu.SemaphoreType.DMA((CHUNKS,)),
            pltpu.SemaphoreType.DMA((n,)),
            pltpu.SemaphoreType.DMA((n,)),
            pltpu.SemaphoreType.DMA((2,)),
            pltpu.SemaphoreType.DMA((2,)),
        ],
        compiler_params=pltpu.CompilerParams(
            collective_id=1, has_side_effects=True, vmem_limit_bytes=VMEM_LIMIT
        ),
    )(slots, grads, mass)


def stack_heads(pair):
    lane = lax.broadcasted_iota(jnp.int32, pair.shape, 1)
    zero = jnp.zeros_like(pair)
    return jnp.concatenate([jnp.where(lane < HD, pair, zero), jnp.where(lane < HD, zero, pair)], 0)


def attend_kernel(
    rank_ref,
    start_ref,
    count_ref,
    query_ref,
    cot_ref,
    recv_ref,
    grad_query_ref,
    grad_ref,
    mass_out_ref,
    keys,
    values,
    grad_keys,
    grad_values,
    mass,
):
    step = pl.program_id(0)
    questions, _, columns = query_ref.shape
    rows = recv_ref.shape[3]
    pairs = columns // LANES
    scale = 1.0 / math.sqrt(HD)

    @pl.when(step == 0)
    def _():
        mass[...] = jnp.zeros_like(mass)

    tail = pl.ds(SLOTS * rows, GROUP * rows)
    keys[tail, :] = jnp.zeros((GROUP * rows, columns), keys.dtype)
    values[tail, :] = jnp.zeros((GROUP * rows, columns), values.dtype)

    def sort_in(s, carry):
        at = pl.ds(pl.multiple_of(rank_ref[s] * rows, rows), rows)
        keys[at, :] = recv_ref[0, s, 0]
        values[at, :] = recv_ref[0, s, 1]
        return carry

    lax.fori_loop(0, SLOTS, sort_in, 0)

    def one(t, carry):
        question = t // pairs
        lanes = pl.ds(pl.multiple_of((t % pairs) * LANES, LANES), LANES)
        start = start_ref[question]
        held = count_ref[question]
        blocks = (held + GROUP - 1) // GROUP

        def run(block_count):
            size = block_count * GROUP * rows
            window = pl.ds(pl.multiple_of(start * rows, rows), size)
            query = stack_heads(query_ref[question, :, lanes] * jnp.asarray(scale, jnp.bfloat16))
            cot = stack_heads(cot_ref[question, :, lanes])
            key = keys[window, lanes]
            value = values[window, lanes]
            last = (((1,), (1,)), ((), ()))
            score = lax.dot_general(key, query, last, preferred_element_type=jnp.float32)
            row = lax.broadcasted_iota(jnp.int32, score.shape, 0)
            score = jnp.where(row < held * rows, score, -jnp.inf)
            exponent = jnp.exp(score - jnp.max(score, 0, keepdims=True))
            prob = exponent * (1.0 / jnp.sum(exponent, 0, keepdims=True))
            rounded = prob.astype(jnp.bfloat16)
            folded = prob.reshape(block_count * GROUP, rows // 8, 8, prob.shape[1]).sum(1)
            mass[pl.ds(start, block_count * GROUP)] += folded
            grad_prob = lax.dot_general(value, cot, last, preferred_element_type=jnp.float32)
            delta = jnp.sum(rounded.astype(jnp.float32) * grad_prob, 0, keepdims=True)
            grad_score = (prob * (grad_prob - delta)).astype(jnp.bfloat16)
            grad_keys[window, lanes] = jnp.dot(
                grad_score, query, preferred_element_type=jnp.float32
            ).astype(jnp.bfloat16)
            grad_values[window, lanes] = jnp.dot(
                rounded, cot, preferred_element_type=jnp.float32
            ).astype(jnp.bfloat16)
            turned = lax.dot_general(
                key, grad_score, (((0,), (0,)), ((), ())), preferred_element_type=jnp.float32
            )
            answer = turned.shape[1] // 2
            both = jnp.concatenate([turned[:HD, :answer], turned[HD:, answer:]], 0)
            grad_query_ref[question, :, lanes] = (both.T * scale).astype(jnp.bfloat16)

        for block_count in range(1, SLOTS // GROUP + 1):
            pl.when(blocks == block_count)(functools.partial(run, block_count))
        return carry

    lax.fori_loop(0, questions * pairs, one, 0)

    def sort_out(s, carry):
        at = pl.ds(pl.multiple_of(rank_ref[s] * rows, rows), rows)
        grad_ref[0, s, 0] = grad_keys[at, :]
        grad_ref[0, s, 1] = grad_values[at, :]
        return carry

    lax.fori_loop(0, SLOTS, sort_out, 0)

    @pl.when(step == pl.num_programs(0) - 1)
    def _():
        def fold(s, carry):
            part = mass[rank_ref[s]]
            mass_out_ref[s] = part[:, :LANES] + part[:, LANES:]
            return carry

        lax.fori_loop(0, SLOTS, fold, 0)


def attend(queries, cotangent, received, rank, starts, counts):
    questions, answer, width = queries.shape
    _, _, _, rows, columns = received.shape
    total = (SLOTS + GROUP) * rows
    side = pl.BlockSpec((questions, answer, columns), lambda c, *_: (0, 0, c))
    tiles = pl.BlockSpec((1, SLOTS, 2, rows, columns), lambda c, *_: (c, 0, 0, 0, 0))
    held = pltpu.VMEM((total, columns), jnp.bfloat16)
    return pl.pallas_call(
        attend_kernel,
        grid_spec=pltpu.PrefetchScalarGridSpec(
            num_scalar_prefetch=3,
            grid=(CHUNKS,),
            in_specs=[side, side, tiles],
            out_specs=(
                side,
                tiles,
                pl.BlockSpec((SLOTS, 8, LANES), lambda c, *_: (0, 0, 0)),
            ),
            scratch_shapes=[
                held,
                held,
                held,
                held,
                pltpu.VMEM((SLOTS + GROUP, 8, 2 * answer), jnp.float32),
            ],
        ),
        out_shape=(
            jax.ShapeDtypeStruct(queries.shape, jnp.bfloat16),
            jax.ShapeDtypeStruct(received.shape, jnp.bfloat16),
            jax.ShapeDtypeStruct((SLOTS, 8, LANES), jnp.float32),
        ),
        compiler_params=pltpu.CompilerParams(vmem_limit_bytes=VMEM_LIMIT),
    )(rank, starts, counts, queries, cotangent, received)


def slot_owners(passage_slot, passage_question, source, decoder, n_devices, per_device, per_pair):
    source_start = source * n_devices * per_device
    table_slot = lax.dynamic_slice_in_dim(
        passage_slot, source_start, n_devices * per_device
    ).reshape(n_devices, per_device)
    table_question = lax.dynamic_slice_in_dim(
        passage_question, source_start, n_devices * per_device
    ).reshape(n_devices, per_device)
    wanted = decoder * per_pair + jnp.arange(per_pair, dtype=jnp.int32)
    matches = table_slot[:, None, :] == wanted[None, :, None]
    owner_ids = jnp.sum(jnp.where(matches, table_question[:, None, :], 0), -1)
    return jnp.where(jnp.any(matches, -1), owner_ids, -1).reshape(n_devices * per_pair)


def body(queries, keys_values, cotangent, passage_slot, passage_question):
    n_devices = lax.axis_size("dp")
    section = lax.axis_index("sec")
    index = lax.axis_index("dp")
    per_device = keys_values.shape[0]
    questions = queries.shape[0]
    per_pair = SLOTS // n_devices
    other_section = 1 - section
    start = (other_section * n_devices + index) * per_device
    slots = lax.dynamic_slice_in_dim(passage_slot, start, per_device)
    numbers = jnp.arange(SLOTS, dtype=jnp.int32)
    places = jnp.arange(per_device, dtype=jnp.int32)
    passage_of = jnp.sum(jnp.where(slots[None, :] == numbers[:, None], places[None, :], 0), -1)
    owners = slot_owners(
        passage_slot, passage_question, other_section, index, n_devices, per_device, per_pair
    )
    order_key = jnp.where(owners < 0, questions, owners) * SLOTS + numbers
    rank = jnp.sum((order_key[None, :] < order_key[:, None]).astype(jnp.int32), -1)
    asked = jnp.arange(questions, dtype=jnp.int32)
    counts = jnp.sum((owners[None, :] == asked[:, None]).astype(jnp.int32), -1)
    starts = jnp.sum((order_key[None, :] < asked[:, None] * SLOTS).astype(jnp.int32), -1)

    received = dispatch(keys_values, passage_of)
    grad_queries, grads, mass = attend(queries, cotangent, received, rank, starts, counts)
    grad_tiles, total = collect(slots, grads, mass, per_device)
    relevance = (jnp.sum(total, (1, 2)) / (HEADS * ANS)).astype(jnp.bfloat16)
    return (grad_queries, grad_tiles, relevance)


def solution(mesh):
    return jax.shard_map(
        body,
        mesh=mesh,
        in_specs=(
            P(("sec", "dp"), None, "mp"),
            P(("sec", "dp"), None, None, "mp"),
            P(("sec", "dp"), None, "mp"),
            P(),
            P(),
        ),
        out_specs=(
            P(("sec", "dp"), None, "mp"),
            P(("sec", "dp"), None, None, "mp"),
            P(("sec", "dp")),
        ),
        check_vma=False,
    )
```

```python
import functools
import math

import jax
import jax.numpy as jnp
from jax import lax
from jax.experimental import pallas as pl
from jax.experimental.pallas import tpu as pltpu
from jax.sharding import PartitionSpec as P

HEADS = 64
HD = 64
ANS = 128
SLOTS = 32
LANES = 128
CHUNKS = 8
GROUP = 4
MESH = pl.DeviceIdType.MESH
VMEM_LIMIT = 48 * 1024 * 1024


def remote(src, dst, send_sem, recv_sem, where):
    return pltpu.make_async_remote_copy(
        src_ref=src,
        dst_ref=dst,
        send_sem=send_sem,
        recv_sem=recv_sem,
        device_id=where,
        device_id_type=MESH,
    )


def greet(targets):
    barrier = pltpu.get_barrier_semaphore()
    for where in targets:
        pl.semaphore_signal(barrier, inc=1, device_id=where, device_id_type=MESH)
    pl.semaphore_wait(barrier, len(targets))


def dispatch_kernel(
    n, index_ref, kv_ref, recv_ref, mid, out, x_send, x_recv, z_send, z_recv, own_sem
):
    section = lax.axis_index("sec")
    me = lax.axis_index("dp")
    per_pair = SLOTS // n
    columns = kv_ref.shape[3] // CHUNKS
    peers = [lax.rem(me + d, n) for d in range(1, n)]
    across = {"sec": 1 - section}
    greet([across] + [{"dp": peer} for peer in peers])

    crossing = []
    for c in range(CHUNKS):
        copy = remote(
            kv_ref.at[:, :, :, pl.ds(c * columns, columns)],
            mid[c],
            x_send.at[c],
            x_recv.at[c],
            across,
        )
        copy.start()
        crossing.append(copy)
    sends = []
    locals_ = []
    my_rows = pl.ds(me * per_pair, per_pair)
    for c in range(CHUNKS):
        crossing[c].wait_recv()

        def place(s, carry):
            out[c, s] = mid[c][index_ref[s]]
            return carry

        lax.fori_loop(0, SLOTS, place, 0)
        for d, peer in enumerate(peers, 1):
            copy = remote(
                out.at[c, pl.ds(peer * per_pair, per_pair)],
                recv_ref.at[c, my_rows],
                z_send.at[c, d],
                z_recv.at[c, d],
                {"dp": peer},
            )
            copy.start()
            sends.append(copy)
        copy = pltpu.make_async_copy(out.at[c, my_rows], recv_ref.at[c, my_rows], own_sem.at[c])
        copy.start()
        locals_.append(copy)
    for c in range(CHUNKS):
        crossing[c].wait_send()
        locals_[c].wait()
        for d in range(1, n):
            source = lax.rem(me + n - d, n)
            landed = recv_ref.at[c, pl.ds(source * per_pair, per_pair)]
            remote(landed, landed, z_send.at[c, d], z_recv.at[c, d], {"dp": source}).wait_recv()
    for copy in sends:
        copy.wait_send()


def dispatch(keys_values, index):
    n = lax.axis_size("dp")
    count, _, rows, width = keys_values.shape
    columns = width // CHUNKS
    return pl.pallas_call(
        functools.partial(dispatch_kernel, n),
        out_shape=jax.ShapeDtypeStruct((CHUNKS, SLOTS, 2, rows, columns), jnp.bfloat16),
        in_specs=[
            pl.BlockSpec(memory_space=pltpu.SMEM),
            pl.BlockSpec(memory_space=pl.ANY),
        ],
        out_specs=pl.BlockSpec(memory_space=pl.ANY),
        scratch_shapes=[
            [pltpu.VMEM((count, 2, rows, columns), jnp.bfloat16)] * CHUNKS,
            pltpu.VMEM((CHUNKS, SLOTS, 2, rows, columns), jnp.bfloat16),
            pltpu.SemaphoreType.DMA((CHUNKS,)),
            pltpu.SemaphoreType.DMA((CHUNKS,)),
            pltpu.SemaphoreType.DMA((CHUNKS, n)),
            pltpu.SemaphoreType.DMA((CHUNKS, n)),
            pltpu.SemaphoreType.DMA((CHUNKS,)),
        ],
        compiler_params=pltpu.CompilerParams(
            collective_id=0, has_side_effects=True, vmem_limit_bytes=VMEM_LIMIT
        ),
    )(index, keys_values)


def collect_kernel(
    n,
    slot_ref,
    grads_ref,
    mass_ref,
    tiles_ref,
    total_ref,
    back,
    dense,
    mass_back,
    mass_dense,
    mass_here,
    mass_other,
    z_send,
    z_recv,
    own_sem,
    x_send,
    x_recv,
    m_send,
    m_recv,
    small_send,
    small_recv,
):
    section = lax.axis_index("sec")
    me = lax.axis_index("dp")
    half = lax.axis_index("mp")
    per_pair = SLOTS // n
    count = dense.shape[1]
    columns = dense.shape[4]
    peers = [lax.rem(me + d, n) for d in range(1, n)]
    across = {"sec": 1 - section}
    beside = {"mp": 1 - half}
    greet([across, beside] + [{"dp": peer} for peer in peers])

    my_rows = pl.ds(me * per_pair, per_pair)
    sends = []
    locals_ = []
    for d, peer in enumerate(peers, 1):
        copy = remote(
            mass_ref.at[pl.ds(peer * per_pair, per_pair)],
            mass_back.at[my_rows],
            m_send.at[d],
            m_recv.at[d],
            {"dp": peer},
        )
        copy.start()
        sends.append(copy)
    own_mass = pltpu.make_async_copy(mass_ref.at[my_rows], mass_back.at[my_rows], own_sem.at[CHUNKS])
    own_mass.start()
    for c in range(CHUNKS):
        for d, peer in enumerate(peers, 1):
            copy = remote(
                grads_ref.at[c, pl.ds(peer * per_pair, per_pair)],
                back[c].at[my_rows],
                z_send.at[c, d],
                z_recv.at[c, d],
                {"dp": peer},
            )
            copy.start()
            sends.append(copy)
        copy = pltpu.make_async_copy(grads_ref.at[c, my_rows], back[c].at[my_rows], own_sem.at[c])
        copy.start()
        locals_.append(copy)

    def arrived(buffer, send_sem, recv_sem, d):
        source = lax.rem(me + n - d, n)
        landed = buffer.at[pl.ds(source * per_pair, per_pair)]
        remote(landed, landed, send_sem, recv_sem, {"dp": source}).wait_recv()

    own_mass.wait()
    for d in range(1, n):
        arrived(mass_back, m_send.at[d], m_recv.at[d], d)

    def pick_mass(j, carry):
        mass_dense[j] = mass_back[slot_ref[j]]
        return carry

    lax.fori_loop(0, count, pick_mass, 0)
    first = remote(mass_dense, mass_here, small_send.at[0], small_recv.at[0], across)
    first.start()

    crossing = []
    second = None
    for c in range(CHUNKS):
        locals_[c].wait()
        for d in range(1, n):
            arrived(back[c], z_send.at[c, d], z_recv.at[c, d], d)

        def pick(j, carry):
            dense[c, j] = back[c][slot_ref[j]]
            return carry

        lax.fori_loop(0, count, pick, 0)
        copy = remote(
            dense.at[c],
            tiles_ref.at[:, :, :, pl.ds(c * columns, columns)],
            x_send.at[c],
            x_recv.at[c],
            across,
        )
        copy.start()
        crossing.append(copy)
        if c == 0:
            first.wait_recv()
            second = remote(mass_here, mass_other, small_send.at[1], small_recv.at[1], beside)
            second.start()
    second.wait()
    total_ref[...] = mass_here[...] + mass_other[...]
    first.wait_send()
    for copy in crossing:
        copy.wait()
    for copy in sends:
        copy.wait_send()


def collect(slots, grads, mass, count):
    n = lax.axis_size("dp")
    _, _, _, rows, columns = grads.shape
    small = pltpu.VMEM((count, 8, LANES), jnp.float32)
    return pl.pallas_call(
        functools.partial(collect_kernel, n),
        out_shape=(
            jax.ShapeDtypeStruct((count, 2, rows, columns * CHUNKS), jnp.bfloat16),
            jax.ShapeDtypeStruct((count, 8, LANES), jnp.float32),
        ),
        in_specs=[
            pl.BlockSpec(memory_space=pltpu.SMEM),
            pl.BlockSpec(memory_space=pl.ANY),
            pl.BlockSpec(memory_space=pl.ANY),
        ],
        out_specs=(
            pl.BlockSpec(memory_space=pl.ANY),
            pl.BlockSpec(memory_space=pltpu.VMEM),
        ),
        scratch_shapes=[
            [pltpu.VMEM((SLOTS, 2, rows, columns), jnp.bfloat16)] * CHUNKS,
            pltpu.VMEM((CHUNKS, count, 2, rows, columns), jnp.bfloat16),
            pltpu.VMEM((SLOTS, 8, LANES), jnp.float32),
            small,
            small,
            small,
            pltpu.SemaphoreType.DMA((CHUNKS, n)),
            pltpu.SemaphoreType.DMA((CHUNKS, n)),
            pltpu.SemaphoreType.DMA((CHUNKS + 1,)),
            pltpu.SemaphoreType.DMA((CHUNKS,)),
            pltpu.SemaphoreType.DMA((CHUNKS,)),
            pltpu.SemaphoreType.DMA((n,)),
            pltpu.SemaphoreType.DMA((n,)),
            pltpu.SemaphoreType.DMA((2,)),
            pltpu.SemaphoreType.DMA((2,)),
        ],
        compiler_params=pltpu.CompilerParams(
            collective_id=1, has_side_effects=True, vmem_limit_bytes=VMEM_LIMIT
        ),
    )(slots, grads, mass)


def stack_heads(pair):
    lane = lax.broadcasted_iota(jnp.int32, pair.shape, 1)
    zero = jnp.zeros_like(pair)
    return jnp.concatenate([jnp.where(lane < HD, pair, zero), jnp.where(lane < HD, zero, pair)], 0)


def attend_kernel(
    rank_ref,
    start_ref,
    count_ref,
    query_ref,
    cot_ref,
    recv_ref,
    grad_query_ref,
    grad_ref,
    mass_out_ref,
    keys,
    values,
    grad_keys,
    grad_values,
    mass,
):
    step = pl.program_id(0)
    questions, _, columns = query_ref.shape
    rows = recv_ref.shape[3]
    pairs = columns // LANES
    scale = 1.0 / math.sqrt(HD)

    @pl.when(step == 0)
    def _():
        mass[...] = jnp.zeros_like(mass)

    tail = pl.ds(SLOTS * rows, GROUP * rows)
    keys[tail, :] = jnp.zeros((GROUP * rows, columns), keys.dtype)
    values[tail, :] = jnp.zeros((GROUP * rows, columns), values.dtype)

    def sort_in(s, carry):
        at = pl.ds(pl.multiple_of(rank_ref[s] * rows, rows), rows)
        keys[at, :] = recv_ref[0, s, 0]
        values[at, :] = recv_ref[0, s, 1]
        return carry

    lax.fori_loop(0, SLOTS, sort_in, 0)

    def one(t, carry):
        question = t // pairs
        lanes = pl.ds(pl.multiple_of((t % pairs) * LANES, LANES), LANES)
        start = start_ref[question]
        held = count_ref[question]
        blocks = (held + GROUP - 1) // GROUP

        def run(block_count):
            size = block_count * GROUP * rows
            window = pl.ds(pl.multiple_of(start * rows, rows), size)
            query = stack_heads(query_ref[question, :, lanes] * jnp.asarray(scale, jnp.bfloat16))
            cot = stack_heads(cot_ref[question, :, lanes])
            key = keys[window, lanes]
            value = values[window, lanes]
            last = (((1,), (1,)), ((), ()))
            score = lax.dot_general(key, query, last, preferred_element_type=jnp.float32)
            row = lax.broadcasted_iota(jnp.int32, score.shape, 0)
            score = jnp.where(row < held * rows, score, -jnp.inf)
            exponent = jnp.exp(score - jnp.max(score, 0, keepdims=True))
            prob = exponent * (1.0 / jnp.sum(exponent, 0, keepdims=True))
            rounded = prob.astype(jnp.bfloat16)
            folded = prob.reshape(block_count * GROUP, rows // 8, 8, prob.shape[1]).sum(1)
            mass[pl.ds(start, block_count * GROUP)] += folded
            grad_prob = lax.dot_general(value, cot, last, preferred_element_type=jnp.float32)
            delta = jnp.sum(rounded.astype(jnp.float32) * grad_prob, 0, keepdims=True)
            grad_score = (prob * (grad_prob - delta)).astype(jnp.bfloat16)
            grad_keys[window, lanes] = jnp.dot(
                grad_score, query, preferred_element_type=jnp.float32
            ).astype(jnp.bfloat16)
            grad_values[window, lanes] = jnp.dot(
                rounded, cot, preferred_element_type=jnp.float32
            ).astype(jnp.bfloat16)
            turned = lax.dot_general(
                key, grad_score, (((0,), (0,)), ((), ())), preferred_element_type=jnp.float32
            )
            answer = turned.shape[1] // 2
            both = jnp.concatenate([turned[:HD, :answer], turned[HD:, answer:]], 0)
            grad_query_ref[question, :, lanes] = (both.T * scale).astype(jnp.bfloat16)

        for block_count in range(1, SLOTS // GROUP + 1):
            pl.when(blocks == block_count)(functools.partial(run, block_count))
        return carry

    lax.fori_loop(0, questions * pairs, one, 0)

    def sort_out(s, carry):
        at = pl.ds(pl.multiple_of(rank_ref[s] * rows, rows), rows)
        grad_ref[0, s, 0] = grad_keys[at, :]
        grad_ref[0, s, 1] = grad_values[at, :]
        return carry

    lax.fori_loop(0, SLOTS, sort_out, 0)

    @pl.when(step == pl.num_programs(0) - 1)
    def _():
        def fold(s, carry):
            part = mass[rank_ref[s]]
            mass_out_ref[s] = part[:, :LANES] + part[:, LANES:]
            return carry

        lax.fori_loop(0, SLOTS, fold, 0)


def attend(queries, cotangent, received, rank, starts, counts):
    questions, answer, width = queries.shape
    _, _, _, rows, columns = received.shape
    total = (SLOTS + GROUP) * rows
    side = pl.BlockSpec((questions, answer, columns), lambda c, *_: (0, 0, c))
    tiles = pl.BlockSpec((1, SLOTS, 2, rows, columns), lambda c, *_: (c, 0, 0, 0, 0))
    held = pltpu.VMEM((total, columns), jnp.bfloat16)
    return pl.pallas_call(
        attend_kernel,
        grid_spec=pltpu.PrefetchScalarGridSpec(
            num_scalar_prefetch=3,
            grid=(CHUNKS,),
            in_specs=[side, side, tiles],
            out_specs=(
                side,
                tiles,
                pl.BlockSpec((SLOTS, 8, LANES), lambda c, *_: (0, 0, 0)),
            ),
            scratch_shapes=[
                held,
                held,
                held,
                held,
                pltpu.VMEM((SLOTS + GROUP, 8, 2 * answer), jnp.float32),
            ],
        ),
        out_shape=(
            jax.ShapeDtypeStruct(queries.shape, jnp.bfloat16),
            jax.ShapeDtypeStruct(received.shape, jnp.bfloat16),
            jax.ShapeDtypeStruct((SLOTS, 8, LANES), jnp.float32),
        ),
        compiler_params=pltpu.CompilerParams(vmem_limit_bytes=VMEM_LIMIT),
    )(rank, starts, counts, queries, cotangent, received)


def slot_owners(passage_slot, passage_question, source, decoder, n_devices, per_device, per_pair):
    source_start = source * n_devices * per_device
    table_slot = lax.dynamic_slice_in_dim(
        passage_slot, source_start, n_devices * per_device
    ).reshape(n_devices, per_device)
    table_question = lax.dynamic_slice_in_dim(
        passage_question, source_start, n_devices * per_device
    ).reshape(n_devices, per_device)
    wanted = decoder * per_pair + jnp.arange(per_pair, dtype=jnp.int32)
    matches = table_slot[:, None, :] == wanted[None, :, None]
    owner_ids = jnp.sum(jnp.where(matches, table_question[:, None, :], 0), -1)
    return jnp.where(jnp.any(matches, -1), owner_ids, -1).reshape(n_devices * per_pair)


def body(queries, keys_values, cotangent, passage_slot, passage_question):
    n_devices = lax.axis_size("dp")
    section = lax.axis_index("sec")
    index = lax.axis_index("dp")
    per_device = keys_values.shape[0]
    questions = queries.shape[0]
    per_pair = SLOTS // n_devices
    other_section = 1 - section
    start = (other_section * n_devices + index) * per_device
    slots = lax.dynamic_slice_in_dim(passage_slot, start, per_device)
    numbers = jnp.arange(SLOTS, dtype=jnp.int32)
    places = jnp.arange(per_device, dtype=jnp.int32)
    passage_of = jnp.sum(jnp.where(slots[None, :] == numbers[:, None], places[None, :], 0), -1)
    owners = slot_owners(
        passage_slot, passage_question, other_section, index, n_devices, per_device, per_pair
    )
    order_key = jnp.where(owners < 0, questions, owners) * SLOTS + numbers
    rank = jnp.sum((order_key[None, :] < order_key[:, None]).astype(jnp.int32), -1)
    asked = jnp.arange(questions, dtype=jnp.int32)
    counts = jnp.sum((owners[None, :] == asked[:, None]).astype(jnp.int32), -1)
    starts = jnp.sum((order_key[None, :] < asked[:, None] * SLOTS).astype(jnp.int32), -1)

    received = dispatch(keys_values, passage_of)
    grad_queries, grads, mass = attend(queries, cotangent, received, rank, starts, counts)
    grad_tiles, total = collect(slots, grads, mass, per_device)
    relevance = (jnp.sum(total, (1, 2)) / (HEADS * ANS)).astype(jnp.bfloat16)
    return (grad_queries, grad_tiles, relevance)


def solution(mesh):
    return jax.shard_map(
        body,
        mesh=mesh,
        in_specs=(
            P(("sec", "dp"), None, "mp"),
            P(("sec", "dp"), None, None, "mp"),
            P(("sec", "dp"), None, "mp"),
            P(),
            P(),
        ),
        out_specs=(
            P(("sec", "dp"), None, "mp"),
            P(("sec", "dp"), None, None, "mp"),
            P(("sec", "dp")),
        ),
        check_vma=False,
    )
```

```python
import functools
import math

import jax
import jax.numpy as jnp
from jax import lax
from jax.experimental import pallas as pl
from jax.experimental.pallas import tpu as pltpu
from jax.sharding import PartitionSpec as P

HEADS = 64
HD = 64
ANS = 128
SLOTS = 32
LANES = 128
CHUNKS = 8
GROUP = 4
AHEAD = 3
MESH = pl.DeviceIdType.MESH
VMEM_LIMIT = 48 * 1024 * 1024


def remote(src, dst, send_sem, recv_sem, where):
    return pltpu.make_async_remote_copy(
        src_ref=src,
        dst_ref=dst,
        send_sem=send_sem,
        recv_sem=recv_sem,
        device_id=where,
        device_id_type=MESH,
    )


def greet(targets):
    barrier = pltpu.get_barrier_semaphore()
    for where in targets:
        pl.semaphore_signal(barrier, inc=1, device_id=where, device_id_type=MESH)
    pl.semaphore_wait(barrier, len(targets))


def dispatch_kernel(
    n, index_ref, kv_ref, recv_ref, mid, out, x_send, x_recv, z_send, z_recv, own_sem
):
    section = lax.axis_index("sec")
    me = lax.axis_index("dp")
    per_pair = SLOTS // n
    columns = kv_ref.shape[3] // CHUNKS
    peers = [lax.rem(me + d, n) for d in range(1, n)]
    across = {"sec": 1 - section}
    greet([across] + [{"dp": peer} for peer in peers])

    crossing = []
    for c in range(CHUNKS):
        copy = remote(
            kv_ref.at[:, :, :, pl.ds(c * columns, columns)],
            mid[c],
            x_send.at[c],
            x_recv.at[c],
            across,
        )
        copy.start()
        crossing.append(copy)
    sends = []
    locals_ = []
    my_rows = pl.ds(me * per_pair, per_pair)
    for c in range(CHUNKS):
        crossing[c].wait_recv()

        def place(s, carry):
            out[c, s] = mid[c][index_ref[s]]
            return carry

        lax.fori_loop(0, SLOTS, place, 0)
        for d, peer in enumerate(peers, 1):
            copy = remote(
                out.at[c, pl.ds(peer * per_pair, per_pair)],
                recv_ref.at[c, my_rows],
                z_send.at[c, d],
                z_recv.at[c, d],
                {"dp": peer},
            )
            copy.start()
            sends.append(copy)
        copy = pltpu.make_async_copy(out.at[c, my_rows], recv_ref.at[c, my_rows], own_sem.at[c])
        copy.start()
        locals_.append(copy)
    for c in range(CHUNKS):
        crossing[c].wait_send()
        locals_[c].wait()
        for d in range(1, n):
            source = lax.rem(me + n - d, n)
            landed = recv_ref.at[c, pl.ds(source * per_pair, per_pair)]
            remote(landed, landed, z_send.at[c, d], z_recv.at[c, d], {"dp": source}).wait_recv()
    for copy in sends:
        copy.wait_send()


def dispatch(keys_values, index):
    n = lax.axis_size("dp")
    count, _, rows, width = keys_values.shape
    columns = width // CHUNKS
    return pl.pallas_call(
        functools.partial(dispatch_kernel, n),
        out_shape=jax.ShapeDtypeStruct((CHUNKS, SLOTS, 2, rows, columns), jnp.bfloat16),
        in_specs=[
            pl.BlockSpec(memory_space=pltpu.SMEM),
            pl.BlockSpec(memory_space=pl.ANY),
        ],
        out_specs=pl.BlockSpec(memory_space=pl.ANY),
        scratch_shapes=[
            [pltpu.VMEM((count, 2, rows, columns), jnp.bfloat16)] * CHUNKS,
            pltpu.VMEM((CHUNKS, SLOTS, 2, rows, columns), jnp.bfloat16),
            pltpu.SemaphoreType.DMA((CHUNKS,)),
            pltpu.SemaphoreType.DMA((CHUNKS,)),
            pltpu.SemaphoreType.DMA((CHUNKS, n)),
            pltpu.SemaphoreType.DMA((CHUNKS, n)),
            pltpu.SemaphoreType.DMA((CHUNKS,)),
        ],
        compiler_params=pltpu.CompilerParams(
            collective_id=0, has_side_effects=True, vmem_limit_bytes=VMEM_LIMIT
        ),
    )(index, keys_values)


def collect_kernel(
    n,
    slot_ref,
    grads_ref,
    mass_ref,
    tiles_ref,
    total_ref,
    back,
    dense,
    mass_back,
    mass_dense,
    mass_here,
    mass_other,
    z_send,
    z_recv,
    own_sem,
    x_send,
    x_recv,
    m_send,
    m_recv,
    small_send,
    small_recv,
):
    section = lax.axis_index("sec")
    me = lax.axis_index("dp")
    half = lax.axis_index("mp")
    per_pair = SLOTS // n
    count = dense.shape[1]
    columns = dense.shape[4]
    peers = [lax.rem(me + d, n) for d in range(1, n)]
    across = {"sec": 1 - section}
    beside = {"mp": 1 - half}
    greet([across, beside] + [{"dp": peer} for peer in peers])

    my_rows = pl.ds(me * per_pair, per_pair)
    sends = []
    locals_ = []
    for d, peer in enumerate(peers, 1):
        copy = remote(
            mass_ref.at[pl.ds(peer * per_pair, per_pair)],
            mass_back.at[my_rows],
            m_send.at[d],
            m_recv.at[d],
            {"dp": peer},
        )
        copy.start()
        sends.append(copy)
    own_mass = pltpu.make_async_copy(mass_ref.at[my_rows], mass_back.at[my_rows], own_sem.at[CHUNKS])
    own_mass.start()

    def start_chunk(c):
        for d, peer in enumerate(peers, 1):
            copy = remote(
                grads_ref.at[c, pl.ds(peer * per_pair, per_pair)],
                back[c].at[my_rows],
                z_send.at[c, d],
                z_recv.at[c, d],
                {"dp": peer},
            )
            copy.start()
            sends.append(copy)
        copy = pltpu.make_async_copy(grads_ref.at[c, my_rows], back[c].at[my_rows], own_sem.at[c])
        copy.start()
        locals_.append(copy)

    for c in range(min(AHEAD, CHUNKS)):
        start_chunk(c)

    def arrived(buffer, send_sem, recv_sem, d):
        source = lax.rem(me + n - d, n)
        landed = buffer.at[pl.ds(source * per_pair, per_pair)]
        remote(landed, landed, send_sem, recv_sem, {"dp": source}).wait_recv()

    own_mass.wait()
    for d in range(1, n):
        arrived(mass_back, m_send.at[d], m_recv.at[d], d)

    def pick_mass(j, carry):
        mass_dense[j] = mass_back[slot_ref[j]]
        return carry

    lax.fori_loop(0, count, pick_mass, 0)
    first = remote(mass_dense, mass_here, small_send.at[0], small_recv.at[0], across)
    first.start()

    crossing = []
    second = None
    for c in range(CHUNKS):
        locals_[c].wait()
        for d in range(1, n):
            arrived(back[c], z_send.at[c, d], z_recv.at[c, d], d)
        if c + AHEAD < CHUNKS:
            start_chunk(c + AHEAD)

        def pick(j, carry):
            dense[c, j] = back[c][slot_ref[j]]
            return carry

        lax.fori_loop(0, count, pick, 0)
        copy = remote(
            dense.at[c],
            tiles_ref.at[:, :, :, pl.ds(c * columns, columns)],
            x_send.at[c],
            x_recv.at[c],
            across,
        )
        copy.start()
        crossing.append(copy)
        if c == 0:
            first.wait_recv()
            second = remote(mass_here, mass_other, small_send.at[1], small_recv.at[1], beside)
            second.start()
    second.wait()
    total_ref[...] = mass_here[...] + mass_other[...]
    first.wait_send()
    for copy in crossing:
        copy.wait()
    for copy in sends:
        copy.wait_send()


def collect(slots, grads, mass, count):
    n = lax.axis_size("dp")
    _, _, _, rows, columns = grads.shape
    small = pltpu.VMEM((count, 8, LANES), jnp.float32)
    return pl.pallas_call(
        functools.partial(collect_kernel, n),
        out_shape=(
            jax.ShapeDtypeStruct((count, 2, rows, columns * CHUNKS), jnp.bfloat16),
            jax.ShapeDtypeStruct((count, 8, LANES), jnp.float32),
        ),
        in_specs=[
            pl.BlockSpec(memory_space=pltpu.SMEM),
            pl.BlockSpec(memory_space=pl.ANY),
            pl.BlockSpec(memory_space=pl.ANY),
        ],
        out_specs=(
            pl.BlockSpec(memory_space=pl.ANY),
            pl.BlockSpec(memory_space=pltpu.VMEM),
        ),
        scratch_shapes=[
            [pltpu.VMEM((SLOTS, 2, rows, columns), jnp.bfloat16)] * CHUNKS,
            pltpu.VMEM((CHUNKS, count, 2, rows, columns), jnp.bfloat16),
            pltpu.VMEM((SLOTS, 8, LANES), jnp.float32),
            small,
            small,
            small,
            pltpu.SemaphoreType.DMA((CHUNKS, n)),
            pltpu.SemaphoreType.DMA((CHUNKS, n)),
            pltpu.SemaphoreType.DMA((CHUNKS + 1,)),
            pltpu.SemaphoreType.DMA((CHUNKS,)),
            pltpu.SemaphoreType.DMA((CHUNKS,)),
            pltpu.SemaphoreType.DMA((n,)),
            pltpu.SemaphoreType.DMA((n,)),
            pltpu.SemaphoreType.DMA((2,)),
            pltpu.SemaphoreType.DMA((2,)),
        ],
        compiler_params=pltpu.CompilerParams(
            collective_id=1, has_side_effects=True, vmem_limit_bytes=VMEM_LIMIT
        ),
    )(slots, grads, mass)


def stack_heads(pair):
    lane = lax.broadcasted_iota(jnp.int32, pair.shape, 1)
    zero = jnp.zeros_like(pair)
    return jnp.concatenate([jnp.where(lane < HD, pair, zero), jnp.where(lane < HD, zero, pair)], 0)


def attend_kernel(
    rank_ref,
    start_ref,
    count_ref,
    query_ref,
    cot_ref,
    recv_ref,
    grad_query_ref,
    grad_ref,
    mass_out_ref,
    keys,
    values,
    grad_keys,
    grad_values,
    mass,
):
    step = pl.program_id(0)
    questions, _, columns = query_ref.shape
    rows = recv_ref.shape[3]
    pairs = columns // LANES
    scale = 1.0 / math.sqrt(HD)

    @pl.when(step == 0)
    def _():
        mass[...] = jnp.zeros_like(mass)

    tail = pl.ds(SLOTS * rows, GROUP * rows)
    keys[tail, :] = jnp.zeros((GROUP * rows, columns), keys.dtype)
    values[tail, :] = jnp.zeros((GROUP * rows, columns), values.dtype)

    def sort_in(s, carry):
        at = pl.ds(pl.multiple_of(rank_ref[s] * rows, rows), rows)
        keys[at, :] = recv_ref[0, s, 0]
        values[at, :] = recv_ref[0, s, 1]
        return carry

    lax.fori_loop(0, SLOTS, sort_in, 0)

    def one(t, carry):
        question = t // pairs
        lanes = pl.ds(pl.multiple_of((t % pairs) * LANES, LANES), LANES)
        start = start_ref[question]
        held = count_ref[question]
        blocks = (held + GROUP - 1) // GROUP

        def run(block_count):
            size = block_count * GROUP * rows
            window = pl.ds(pl.multiple_of(start * rows, rows), size)
            query = stack_heads(query_ref[question, :, lanes] * jnp.asarray(scale, jnp.bfloat16))
            cot = stack_heads(cot_ref[question, :, lanes])
            key = keys[window, lanes]
            value = values[window, lanes]
            last = (((1,), (1,)), ((), ()))
            score = lax.dot_general(key, query, last, preferred_element_type=jnp.float32)
            row = lax.broadcasted_iota(jnp.int32, score.shape, 0)
            score = jnp.where(row < held * rows, score, -jnp.inf)
            exponent = jnp.exp(score - jnp.max(score, 0, keepdims=True))
            prob = exponent * (1.0 / jnp.sum(exponent, 0, keepdims=True))
            rounded = prob.astype(jnp.bfloat16)
            folded = prob.reshape(block_count * GROUP, rows // 8, 8, prob.shape[1]).sum(1)
            mass[pl.ds(start, block_count * GROUP)] += folded
            grad_prob = lax.dot_general(value, cot, last, preferred_element_type=jnp.float32)
            delta = jnp.sum(rounded.astype(jnp.float32) * grad_prob, 0, keepdims=True)
            grad_score = (prob * (grad_prob - delta)).astype(jnp.bfloat16)
            grad_keys[window, lanes] = jnp.dot(
                grad_score, query, preferred_element_type=jnp.float32
            ).astype(jnp.bfloat16)
            grad_values[window, lanes] = jnp.dot(
                rounded, cot, preferred_element_type=jnp.float32
            ).astype(jnp.bfloat16)
            turned = lax.dot_general(
                key, grad_score, (((0,), (0,)), ((), ())), preferred_element_type=jnp.float32
            )
            answer = turned.shape[1] // 2
            both = jnp.concatenate([turned[:HD, :answer], turned[HD:, answer:]], 0)
            grad_query_ref[question, :, lanes] = (both.T * scale).astype(jnp.bfloat16)

        for block_count in range(1, SLOTS // GROUP + 1):
            pl.when(blocks == block_count)(functools.partial(run, block_count))
        return carry

    lax.fori_loop(0, questions * pairs, one, 0)

    def sort_out(s, carry):
        at = pl.ds(pl.multiple_of(rank_ref[s] * rows, rows), rows)
        grad_ref[0, s, 0] = grad_keys[at, :]
        grad_ref[0, s, 1] = grad_values[at, :]
        return carry

    lax.fori_loop(0, SLOTS, sort_out, 0)

    @pl.when(step == pl.num_programs(0) - 1)
    def _():
        def fold(s, carry):
            part = mass[rank_ref[s]]
            mass_out_ref[s] = part[:, :LANES] + part[:, LANES:]
            return carry

        lax.fori_loop(0, SLOTS, fold, 0)


def attend(queries, cotangent, received, rank, starts, counts):
    questions, answer, width = queries.shape
    _, _, _, rows, columns = received.shape
    total = (SLOTS + GROUP) * rows
    side = pl.BlockSpec((questions, answer, columns), lambda c, *_: (0, 0, c))
    tiles = pl.BlockSpec((1, SLOTS, 2, rows, columns), lambda c, *_: (c, 0, 0, 0, 0))
    held = pltpu.VMEM((total, columns), jnp.bfloat16)
    return pl.pallas_call(
        attend_kernel,
        grid_spec=pltpu.PrefetchScalarGridSpec(
            num_scalar_prefetch=3,
            grid=(CHUNKS,),
            in_specs=[side, side, tiles],
            out_specs=(
                side,
                tiles,
                pl.BlockSpec((SLOTS, 8, LANES), lambda c, *_: (0, 0, 0)),
            ),
            scratch_shapes=[
                held,
                held,
                held,
                held,
                pltpu.VMEM((SLOTS + GROUP, 8, 2 * answer), jnp.float32),
            ],
        ),
        out_shape=(
            jax.ShapeDtypeStruct(queries.shape, jnp.bfloat16),
            jax.ShapeDtypeStruct(received.shape, jnp.bfloat16),
            jax.ShapeDtypeStruct((SLOTS, 8, LANES), jnp.float32),
        ),
        compiler_params=pltpu.CompilerParams(vmem_limit_bytes=VMEM_LIMIT),
    )(rank, starts, counts, queries, cotangent, received)


def slot_owners(passage_slot, passage_question, source, decoder, n_devices, per_device, per_pair):
    source_start = source * n_devices * per_device
    table_slot = lax.dynamic_slice_in_dim(
        passage_slot, source_start, n_devices * per_device
    ).reshape(n_devices, per_device)
    table_question = lax.dynamic_slice_in_dim(
        passage_question, source_start, n_devices * per_device
    ).reshape(n_devices, per_device)
    wanted = decoder * per_pair + jnp.arange(per_pair, dtype=jnp.int32)
    matches = table_slot[:, None, :] == wanted[None, :, None]
    owner_ids = jnp.sum(jnp.where(matches, table_question[:, None, :], 0), -1)
    return jnp.where(jnp.any(matches, -1), owner_ids, -1).reshape(n_devices * per_pair)


def body(queries, keys_values, cotangent, passage_slot, passage_question):
    n_devices = lax.axis_size("dp")
    section = lax.axis_index("sec")
    index = lax.axis_index("dp")
    per_device = keys_values.shape[0]
    questions = queries.shape[0]
    per_pair = SLOTS // n_devices
    other_section = 1 - section
    start = (other_section * n_devices + index) * per_device
    slots = lax.dynamic_slice_in_dim(passage_slot, start, per_device)
    numbers = jnp.arange(SLOTS, dtype=jnp.int32)
    places = jnp.arange(per_device, dtype=jnp.int32)
    passage_of = jnp.sum(jnp.where(slots[None, :] == numbers[:, None], places[None, :], 0), -1)
    owners = slot_owners(
        passage_slot, passage_question, other_section, index, n_devices, per_device, per_pair
    )
    order_key = jnp.where(owners < 0, questions, owners) * SLOTS + numbers
    rank = jnp.sum((order_key[None, :] < order_key[:, None]).astype(jnp.int32), -1)
    asked = jnp.arange(questions, dtype=jnp.int32)
    counts = jnp.sum((owners[None, :] == asked[:, None]).astype(jnp.int32), -1)
    starts = jnp.sum((order_key[None, :] < asked[:, None] * SLOTS).astype(jnp.int32), -1)

    received = dispatch(keys_values, passage_of)
    grad_queries, grads, mass = attend(queries, cotangent, received, rank, starts, counts)
    grad_tiles, total = collect(slots, grads, mass, per_device)
    relevance = (jnp.sum(total, (1, 2)) / (HEADS * ANS)).astype(jnp.bfloat16)
    return (grad_queries, grad_tiles, relevance)


def solution(mesh):
    return jax.shard_map(
        body,
        mesh=mesh,
        in_specs=(
            P(("sec", "dp"), None, "mp"),
            P(("sec", "dp"), None, None, "mp"),
            P(("sec", "dp"), None, "mp"),
            P(),
            P(),
        ),
        out_specs=(
            P(("sec", "dp"), None, "mp"),
            P(("sec", "dp"), None, None, "mp"),
            P(("sec", "dp")),
        ),
        check_vma=False,
    )
```
